512 devices in a mesh: dp: 32 (over x, y, core), vocab: 16 (over z).
Axes of the slice: x: 4, y: 4, z: 16, core: 2. Of those that a mesh axis runs over, the one named last changes fastest.
Arguments:
- hidden: float32 [64, 4608], P('dp'), may hold values from -6 to 6
- norm_gain: float32 [4608], replicated, may hold values from 0.5 to 1.5
- embed_table: bfloat16 [196608, 4608], P(('dp', 'vocab')), as said below
- tokens: int32 [64, 3], replicated, may hold values from 0 to 196607, as said below
Outputs:
- log_probs: float32 [64, 3], P('dp')
- final_hidden: float32 [64, 4608], P('dp')
The draws below stay inside these ranges and needn't reach their ends.
Inputs may be any that keep to these rules, and one draw needn't show every extreme that they name: `tokens`: token ids are vocabulary entries. `embed_table`: entries lie between -21 / sqrt(4608) and 21 / sqrt(4608).
All inputs are finite; a program needn't handle non-finite values.
Results may differ from the reference program's by a relative error of at most 0.0003.
Values may be sent and summed in bfloat16 or wider, within the bound.
No kernel may reach another device: no remote copies, remote signals or barrier semaphores. Data moves between devices by JAX's collectives and lax.ppermute only.
A program may use at most 64 MiB of HBM per device.

```python
import math
import jax
import jax.numpy as jnp
from jax import lax

D = 4608
VOC_DEV = 384
B_DEV = 2
STEPS = 3
B = 64
VOCAB = 196608
N_DP = 32
N_VOCAB = 16


def draw_tokens(key, part):
    key_owner = jax.random.fold_in(key, 11)
    key_local = jax.random.fold_in(key, 23)
    devices_all = N_DP * N_VOCAB
    owner = jax.random.randint(key_owner, (B, STEPS), 0, devices_all, dtype=jnp.int32)
    summary = lax_iota_rows()
    group_index = summary // B_DEV
    step_index = jnp.arange(STEPS, dtype=jnp.int32)[None, :]
    far_owner = (group_index + N_DP // 2) % N_DP * N_VOCAB + (group_index + step_index) % N_VOCAB
    chosen = jnp.where(summary % B_DEV == 0, far_owner, owner)
    local_row = jax.random.randint(key_local, (B, STEPS), 0, VOC_DEV, dtype=jnp.int32)
    return (chosen * VOC_DEV + local_row).astype(jnp.int32)


def lax_iota_rows():
    return jnp.arange(B, dtype=jnp.int32)[:, None]


def draw_embed_table(key, part):
    key_level = jax.random.fold_in(key, 31)
    key_row = jax.random.fold_in(key, 37)
    key_entry = jax.random.fold_in(key, 41)
    blocks = VOCAB // VOC_DEV
    level = jnp.exp(jax.random.uniform(key_level, (blocks, 1, 1), jnp.float32, -3.0, 0.18))
    entries = jax.random.truncated_normal(key_entry, -4.0, 4.0, (blocks, VOC_DEV, D), jnp.float32)
    row_factor = jnp.exp(jax.random.uniform(key_row, (blocks, VOC_DEV, 1), jnp.float32, -0.35, 0.35))
    table = entries * level * row_factor * (3.0 / math.sqrt(D))
    return table.reshape(VOCAB, D).astype(jnp.bfloat16)


def block_scale(own_key, extent, cuts, least, top_value):
    factor_of, own = 1.0, jax.random.fold_in(own_key, 6)
    for dim, blocks in cuts:
        steps = jnp.exp(jax.random.uniform(jax.random.fold_in(own, dim), (blocks,), jnp.float32, least / len(cuts), top_value / len(cuts)))
        factor_of = factor_of * jnp.repeat(steps, extent[dim] // blocks).reshape([-1 if axis == dim else 1 for axis in range(len(extent))])
    return factor_of


def centred(rng, shape, spread, limit, cuts=(), held_as=jnp.bfloat16):
    loudness = block_scale(rng, shape, cuts, -0.22, 0.18) if cuts else 1.0
    values = jax.random.normal(rng, shape, jnp.float32) * spread * loudness
    return jnp.minimum(jnp.maximum(values, -limit), limit).astype(held_as)


def setup_inputs(seed: int = 0) -> dict:
    keys = jax.random.split(jax.random.key(seed), 5)
    return {
        "hidden": centred(keys[0], (B, D), 1.0, 6.0, ((0, 32),), jnp.float32),
        "norm_gain": jnp.clip(1.0 + 0.1 * jax.random.normal(keys[1], (D,), jnp.float32), 0.5, 1.5),
        "embed_table": draw_embed_table(jax.random.fold_in(keys[4], 71), 0),
        "tokens": draw_tokens(jax.random.fold_in(keys[4], 71), 0),
    }


epsilon_value = 1e-06
softcap_value = 30.0

def reference(hidden, norm_gain, embed_table, tokens):
    current = hidden
    scale_factor = math.sqrt(D)
    results = []
    for decode_step in range(STEPS):
        token_ids = tokens[:, decode_step].astype(jnp.int32)
        square_mean = lax.optimization_barrier(jnp.mean(current * current, axis=-1, keepdims=True))
        normed = (current * lax.rsqrt(square_mean + epsilon_value) * norm_gain).astype(jnp.bfloat16)
        logits = lax.dot_general(normed, embed_table, (((1,), (1,)), ((), ())), preferred_element_type=jnp.float32)
        capped = softcap_value * jnp.tanh(logits / softcap_value)
        exp_total = lax.optimization_barrier(jnp.sum(jnp.exp(capped), axis=-1))
        target = jnp.take_along_axis(capped, token_ids[:, None], axis=1)[:, 0]
        results.append(target - jnp.log(exp_total))
        looked = jnp.take(embed_table, token_ids, axis=0).astype(jnp.float32)
        current = current + scale_factor * looked
    return (jnp.stack(results, axis=1), current)
```

```python
import math

import jax
import jax.numpy as jnp
from jax import lax
from jax.sharding import Mesh
from jax.sharding import PartitionSpec as P

D = 4608
STEPS = 3
XY = ("dp_0", "dp_1")
DP = ("dp_0", "dp_1", "dp_2")
DP_VOCAB = ("dp_0", "dp_1", "dp_2", "vocab")
SLOTS = 8

epsilon_value = 1e-06
softcap_value = 30.0


def exchange(x, axis):
    return lax.all_to_all(x, axis, split_axis=0, concat_axis=0, tiled=True)


def to_each(x, axis):
    return exchange(jnp.broadcast_to(x[None], (lax.axis_size(axis), *x.shape)), axis)


def other_core(x):
    return lax.ppermute(x, "dp_2", [(0, 1), (1, 0)])


def in_three(x):
    high = lax.reduce_precision(x, 8, 7)
    middle = lax.reduce_precision(x - high, 8, 7)
    return jnp.concatenate([high, middle, x - high - middle], axis=-1).astype(jnp.bfloat16)


def on_device(hidden, norm_gain, embed_table, tokens):
    own_rows = hidden.shape[0]
    shard_rows = embed_table.shape[0]
    n_xy = lax.axis_size(XY)
    core = lax.axis_index("dp_2")
    shard_start = (
        lax.axis_index(DP) * lax.axis_size("vocab") + lax.axis_index("vocab")
    ) * shard_rows
    scale_factor = math.sqrt(D)
    used = STEPS * own_rows

    ids = jnp.transpose(tokens.reshape(n_xy, 2, own_rows, STEPS), (1, 0, 3, 2))
    ids = ids.reshape(2, n_xy, used) - shard_start
    ids = jnp.pad(ids, ((0, 0), (0, 0), (0, SLOTS - used)), constant_values=-1)
    mine = jnp.where(core == 0, ids[0], ids[1]).reshape(n_xy * SLOTS)
    theirs = jnp.where(core == 0, ids[1], ids[0]).reshape(n_xy * SLOTS)
    columns = lax.broadcasted_iota(jnp.int32, (1, shard_rows), 1)
    match_mine = mine[:, None] == columns
    match_theirs = theirs[:, None] == columns

    def rows_of(match):
        return jnp.dot(
            match.astype(jnp.bfloat16), embed_table, preferred_element_type=jnp.float32
        ).astype(jnp.bfloat16)

    arriving = other_core(rows_of(match_theirs))
    found = (rows_of(match_mine) + arriving).reshape(n_xy, SLOTS, D)
    held = exchange(found, XY).astype(jnp.float32).sum(axis=0).astype(jnp.bfloat16)
    first = to_each(held[: 2 * own_rows], "vocab").astype(jnp.float32).sum(axis=0)

    currents = [hidden]
    for step in range(2):
        looked = first[step * own_rows : (step + 1) * own_rows]
        currents.append(currents[-1] + scale_factor * looked)
    states = jnp.concatenate(currents, axis=0)
    square_mean = jnp.mean(states * states, axis=-1, keepdims=True)
    normed = (states * lax.rsqrt(square_mean + epsilon_value) * norm_gain).astype(jnp.bfloat16)
    normed = jnp.pad(normed, ((0, SLOTS - used), (0, 0)))
    of_mine = to_each(normed, XY).reshape(n_xy * SLOTS, D)
    of_theirs = other_core(of_mine)

    def totals(rows, match):
        logits = lax.dot_general(
            rows, embed_table, (((1,), (1,)), ((), ())), preferred_element_type=jnp.float32
        )
        capped = softcap_value * jnp.tanh(logits / softcap_value)
        exp_total = jnp.sum(jnp.exp(capped), axis=-1)
        target = jnp.sum(jnp.where(match, capped, 0.0), axis=-1)
        return jnp.concatenate(
            [exp_total.reshape(n_xy, SLOTS), target.reshape(n_xy, SLOTS)], axis=1
        )

    for_mine = totals(of_mine, match_mine)
    for_theirs = totals(of_theirs, match_theirs)
    for_0 = jnp.where(core == 0, for_mine, for_theirs)
    for_1 = jnp.where(core == 0, for_theirs, for_mine)
    parts = jnp.stack([for_0, for_1], axis=1).reshape(2 * n_xy, 1, 2 * SLOTS)
    parts = jnp.pad(parts, ((0, 0), (0, 0), (0, 128 - 2 * SLOTS)))
    part = exchange(parts, DP).sum(axis=0)[:, : 2 * SLOTS]
    part = jnp.pad(in_three(part), ((0, own_rows - 1), (0, 128 - 6 * SLOTS)))
    last = jnp.concatenate([held[2 * own_rows : used], part], axis=1)
    last = to_each(last, "vocab").astype(jnp.float32).sum(axis=0)
    whole = last[0, D : D + 6 * SLOTS].reshape(3, 2, SLOTS).sum(axis=0)
    log_probs = whole[1, :used] - jnp.log(whole[0, :used])
    final_hidden = currents[2] + scale_factor * last[:, :D]
    return (jnp.transpose(log_probs.reshape(STEPS, own_rows)), final_hidden)


def solution(mesh):
    finer = Mesh(
        mesh.devices.reshape(4, 4, 2, mesh.shape["vocab"]), ("dp_0", "dp_1", "dp_2", "vocab")
    )
    in_specs = (P(DP, None), P(), P(DP_VOCAB, None), P())
    out_specs = (P(DP, None), P(DP, None))
    return jax.shard_map(
        on_device, mesh=finer, in_specs=in_specs, out_specs=out_specs, check_vma=False
    )
```

```python
import math

import jax
import jax.numpy as jnp
from jax import lax
from jax.sharding import Mesh
from jax.sharding import PartitionSpec as P

D = 4608
STEPS = 3
XY = ("dp_0", "dp_1")
DP = ("dp_0", "dp_1", "dp_2")
DP_VOCAB = ("dp_0", "dp_1", "dp_2", "vocab")
SLOTS = 8

epsilon_value = 1e-06
softcap_value = 30.0


def exchange(x, axis):
    return lax.all_to_all(x, axis, split_axis=0, concat_axis=0, tiled=True)


def to_each(x, axis):
    return exchange(jnp.broadcast_to(x[None], (lax.axis_size(axis), *x.shape)), axis)


def other_core(x):
    return lax.ppermute(x, "dp_2", [(0, 1), (1, 0)])


def on_device(hidden, norm_gain, embed_table, tokens):
    own_rows = hidden.shape[0]
    shard_rows = embed_table.shape[0]
    n_xy = lax.axis_size(XY)
    core = lax.axis_index("dp_2")
    shard_start = (
        lax.axis_index(DP) * lax.axis_size("vocab") + lax.axis_index("vocab")
    ) * shard_rows
    scale_factor = math.sqrt(D)
    used = STEPS * own_rows

    ids = jnp.transpose(tokens.reshape(n_xy, 2, own_rows, STEPS), (1, 0, 3, 2))
    ids = ids.reshape(2, n_xy, used) - shard_start
    ids = jnp.pad(ids, ((0, 0), (0, 0), (0, SLOTS - used)), constant_values=-1)
    mine = jnp.where(core == 0, ids[0], ids[1]).reshape(n_xy * SLOTS)
    theirs = jnp.where(core == 0, ids[1], ids[0]).reshape(n_xy * SLOTS)
    columns = lax.broadcasted_iota(jnp.int32, (1, shard_rows), 1)
    match_mine = mine[:, None] == columns
    match_theirs = theirs[:, None] == columns

    def rows_of(match):
        return jnp.dot(
            match.astype(jnp.bfloat16), embed_table, preferred_element_type=jnp.float32
        ).astype(jnp.bfloat16)

    arriving = other_core(rows_of(match_theirs))
    found = (rows_of(match_mine) + arriving).reshape(n_xy, SLOTS, D)
    held = exchange(found, XY).astype(jnp.float32).sum(axis=0).astype(jnp.bfloat16)
    looked = lax.all_gather(held[:used].reshape(STEPS, own_rows, D), "vocab")
    looked = looked.astype(jnp.float32).sum(axis=0)

    currents = [hidden]
    for step in range(STEPS):
        currents.append(currents[-1] + scale_factor * looked[step])
    states = jnp.concatenate(currents[:STEPS], axis=0)
    square_mean = jnp.mean(states * states, axis=-1, keepdims=True)
    normed = (states * lax.rsqrt(square_mean + epsilon_value) * norm_gain).astype(jnp.bfloat16)
    normed = jnp.pad(normed, ((0, SLOTS - used), (0, 0)))
    of_mine = to_each(normed, XY).reshape(n_xy * SLOTS, D)
    of_theirs = other_core(of_mine)

    def totals(rows, match):
        logits = lax.dot_general(
            rows, embed_table, (((1,), (1,)), ((), ())), preferred_element_type=jnp.float32
        )
        capped = softcap_value * jnp.tanh(logits / softcap_value)
        exp_total = jnp.sum(jnp.exp(capped), axis=-1)
        target = jnp.sum(jnp.where(match, capped, 0.0), axis=-1)
        return jnp.stack([exp_total, target])

    for_mine = totals(of_mine, match_mine)
    for_theirs = totals(of_theirs, match_theirs)
    halves = jnp.where(
        core == 0, jnp.stack([for_mine, for_theirs]), jnp.stack([for_theirs, for_mine])
    )
    parts = jnp.broadcast_to(halves[None], (n_xy, *halves.shape))
    part = exchange(parts.reshape(2 * n_xy, *halves.shape[1:]), DP).sum(axis=0)
    whole = to_each(part, "vocab").sum(axis=0)
    log_probs = whole[1] - jnp.log(whole[0])
    log_probs = lax.dynamic_slice_in_dim(log_probs, lax.axis_index(XY) * SLOTS, used)
    return (jnp.transpose(log_probs.reshape(STEPS, own_rows)), currents[STEPS])


def solution(mesh):
    finer = Mesh(
        mesh.devices.reshape(4, 4, 2, mesh.shape["vocab"]), ("dp_0", "dp_1", "dp_2", "vocab")
    )
    in_specs = (P(DP, None), P(), P(DP_VOCAB, None), P())
    out_specs = (P(DP, None), P(DP, None))
    return jax.shard_map(
        on_device, mesh=finer, in_specs=in_specs, out_specs=out_specs, check_vma=False
    )
```

```python
import functools
import math

import jax
import jax.numpy as jnp
from jax import lax
from jax.experimental import pallas as pl
from jax.experimental.pallas import tpu as pltpu
from jax.sharding import Mesh
from jax.sharding import PartitionSpec as P

D = 4608
STEPS = 3
XY = ("dp_0", "dp_1")
DP = ("dp_0", "dp_1", "dp_2")
DP_VOCAB = ("dp_0", "dp_1", "dp_2", "vocab")
ROOM = 2
SLOTS = 8

epsilon_value = 1e-06
softcap_value = 30.0


def exchange(x, axis):
    return lax.all_to_all(x, axis, split_axis=0, concat_axis=0, tiled=True)


def to_each(x, axis):
    return exchange(jnp.broadcast_to(x[None], (lax.axis_size(axis), *x.shape)), axis)


def other_core(x):
    return lax.ppermute(x, "dp_2", [(0, 1), (1, 0)])


def picked(block, index):
    rows = lax.broadcasted_iota(jnp.int32, block.shape, 0)
    return jnp.sum(jnp.where(rows == index, block.astype(jnp.float32), 0.0), axis=0, keepdims=True)


def placed(row, index, count):
    rows = lax.broadcasted_iota(jnp.int32, (count, row.shape[1]), 0)
    return jnp.where(rows == index, row, 0.0)


def lookup_kernel(turn, tokens, table, rows, ids, held, found, sem):
    steps, summaries = tokens.shape
    shard_rows = table.shape[0]
    own_rows = summaries // rows.shape[0]
    start = (
        lax.axis_index(DP) * lax.axis_size("vocab") + lax.axis_index("vocab")
    ) * shard_rows
    core = lax.axis_index("dp_2")
    copy = pltpu.make_async_copy(table, held, sem)
    copy.start()
    rows[...] = jnp.zeros_like(rows)
    half_of = lax.broadcasted_iota(jnp.int32, ids.shape, 0)
    lane_of = lax.broadcasted_iota(jnp.int32, ids.shape, 1)

    def scan(group, state):
        n, all_ids = state
        count = jnp.int32(0)
        half = jnp.where(group % 2 == core, 0, 1)
        for step in range(steps):
            for row in range(own_rows):
                local = tokens[step, group * own_rows + row] - start
                lane = group // 2 * SLOTS + step * own_rows + row
                all_ids = jnp.where((half_of == half) & (lane_of == lane), local, all_ids)
                here = (local >= 0) & (local < shard_rows)
                place = count - turn[0] * ROOM
                now = here & (place >= 0) & (place < ROOM)

                @pl.when(now)
                def _():
                    found[3 * n] = local
                    found[3 * n + 1] = group
                    found[3 * n + 2] = place

                n = n + now.astype(jnp.int32)
                count = count + here.astype(jnp.int32)
        return n, all_ids

    n, all_ids = lax.fori_loop(
        0, rows.shape[0], scan, (jnp.int32(0), jnp.full(ids.shape, -1, jnp.int32))
    )
    ids[...] = all_ids
    copy.wait()

    def give(i, _):
        local, group, place = found[3 * i], found[3 * i + 1], found[3 * i + 2]
        block = held[pl.ds(pl.multiple_of(local // 16 * 16, 16), 16), :]
        row = placed(picked(block, local % 16), place, ROOM)
        rows[group] = (rows[group].astype(jnp.float32) + row).astype(jnp.bfloat16)
        return 0

    lax.fori_loop(0, n, give, 0)


def own_tokens(tokens, own_rows, shard_rows):
    group = lax.axis_index(DP)
    holders, order = [], []
    for step in range(tokens.shape[0]):
        for row in range(own_rows):
            holder = tokens[step, group * own_rows + row] // shard_rows
            order.append(sum(((holder == h).astype(jnp.int32) for h in holders), jnp.int32(0)))
            holders.append(holder)
    return holders, order


def collect_kernel(shard_rows, turn, tokens, rows, out, buffer, sems):
    own_rows = out.shape[1]
    n_vocab = lax.axis_size("vocab")
    holders, order = own_tokens(tokens, own_rows, shard_rows)
    out[...] = jnp.zeros_like(out)
    wanted, copies = [], []
    for i, (holder, place) in enumerate(zip(holders, order)):
        wanted.append(
            (holder % n_vocab == lax.axis_index("vocab")) & (place // ROOM == turn[0])
        )
        copies.append(
            pltpu.make_async_copy(rows.at[holder // n_vocab], buffer.at[i], sems.at[i])
        )
        pl.when(wanted[i])(copies[i].start)
    for i, place in enumerate(order):

        @pl.when(wanted[i])
        def _():
            copies[i].wait()
            row = placed(picked(buffer[i], place % ROOM), i % own_rows, own_rows)
            step = i // own_rows
            out[step] = (out[step].astype(jnp.float32) + row).astype(jnp.bfloat16)


def norm_kernel(shard_rows, tokens, looked, hidden, gain, normed, final, buffer, sems):
    steps, own_rows, _ = looked.shape[1:]
    n_vocab = lax.axis_size("vocab")
    holders, _ = own_tokens(tokens, own_rows, shard_rows)
    copies = []
    for i, holder in enumerate(holders):
        copies.append(
            pltpu.make_async_copy(
                looked.at[holder % n_vocab, i // own_rows], buffer.at[i], sems.at[i]
            )
        )
        copies[i].start()
    current = hidden[...]
    states = []
    for step in range(steps):
        square_mean = jnp.mean(current * current, axis=-1, keepdims=True)
        states.append(current * lax.rsqrt(square_mean + epsilon_value) * gain[...])
        row_of = lax.broadcasted_iota(jnp.int32, current.shape, 0)
        here = jnp.zeros_like(current)
        for row in range(own_rows):
            copies[step * own_rows + row].wait()
            block = buffer[step * own_rows + row].astype(jnp.float32)
            here = jnp.where(row_of == row, block, here)
        current = current + math.sqrt(D) * here
    final[...] = current
    empty = jnp.zeros((SLOTS - steps * own_rows, D), jnp.float32)
    normed[...] = jnp.concatenate([*states, empty], axis=0).astype(jnp.bfloat16)


def on_chip(kernel, out_shape, scratch, *operands):
    return pl.pallas_call(
        kernel,
        out_shape=out_shape,
        in_specs=[pl.BlockSpec(memory_space=space) for _, space in operands],
        out_specs=jax.tree.map(lambda _: pl.BlockSpec(memory_space=pltpu.VMEM), out_shape),
        scratch_shapes=scratch,
        compiler_params=pltpu.CompilerParams(vmem_limit_bytes=20 * 2**20),
    )(*(x for x, _ in operands))


def on_device(hidden, norm_gain, embed_table, tokens):
    own_rows = hidden.shape[0]
    shard_rows = embed_table.shape[0]
    n_xy, n_groups, n_vocab = lax.axis_size(XY), lax.axis_size(DP), lax.axis_size("vocab")
    core = lax.axis_index("dp_2")
    used = STEPS * own_rows
    columns = lax.broadcasted_iota(jnp.int32, (1, shard_rows), 1)
    by_step = jnp.transpose(tokens)
    bf16, f32 = jnp.bfloat16, jnp.float32

    def sent(turn):
        turn = jnp.full((1,), turn, jnp.int32)
        rows, ids = on_chip(
            lookup_kernel,
            (
                jax.ShapeDtypeStruct((n_groups, ROOM, D), bf16),
                jax.ShapeDtypeStruct((2, n_xy * SLOTS), jnp.int32),
            ),
            [
                pltpu.VMEM(embed_table.shape, bf16),
                pltpu.SMEM((3 * n_groups * used,), jnp.int32),
                pltpu.SemaphoreType.DMA,
            ],
            (turn, pltpu.SMEM),
            (by_step, pltpu.SMEM),
            (embed_table, pl.ANY),
        )
        rows = exchange(rows, DP)
        held = on_chip(
            functools.partial(collect_kernel, shard_rows),
            jax.ShapeDtypeStruct((STEPS, own_rows, D), bf16),
            [pltpu.VMEM((used, ROOM, D), bf16), pltpu.SemaphoreType.DMA((used,))],
            (turn, pltpu.SMEM),
            (by_step, pltpu.SMEM),
            (rows, pl.ANY),
        )
        return held, ids

    holder = by_step // shard_rows
    pairs = holder.reshape(STEPS, n_groups, own_rows)
    same = jnp.zeros((STEPS, n_groups, own_rows), jnp.int32)
    for step in range(STEPS):
        for row in range(own_rows):
            same = same + (pairs == pairs[step : step + 1, :, row : row + 1]).astype(jnp.int32)
    turns = (jnp.max(same) + ROOM - 1) // ROOM

    held, ids = sent(0)
    _, held = lax.while_loop(
        lambda state: state[0] < turns,
        lambda state: (state[0] + 1, state[1] + sent(state[0])[0]),
        (jnp.int32(1), held),
    )
    looked = lax.all_gather(held, "vocab")
    normed, final_hidden = on_chip(
        functools.partial(norm_kernel, shard_rows),
        (
            jax.ShapeDtypeStruct((SLOTS, D), bf16),
            jax.ShapeDtypeStruct((own_rows, D), f32),
        ),
        [pltpu.VMEM((used, own_rows, D), bf16), pltpu.SemaphoreType.DMA((used,))],
        (by_step, pltpu.SMEM),
        (looked, pl.ANY),
        (hidden, pltpu.VMEM),
        (norm_gain.reshape(1, D), pltpu.VMEM),
    )
    match_mine = ids[0][:, None] == columns
    match_theirs = ids[1][:, None] == columns

    of_mine = to_each(normed, XY).reshape(n_xy * SLOTS, D)
    of_theirs = other_core(of_mine)

    def totals(rows, match):
        logits = lax.dot_general(
            rows, embed_table, (((1,), (1,)), ((), ())), preferred_element_type=jnp.float32
        )
        capped = softcap_value * jnp.tanh(logits / softcap_value)
        exp_total = jnp.sum(jnp.exp(capped), axis=-1)
        target = jnp.sum(jnp.where(match, capped, 0.0), axis=-1)
        return jnp.stack([exp_total, target])

    for_mine = totals(of_mine, match_mine)
    for_theirs = totals(of_theirs, match_theirs)
    halves = jnp.where(
        core == 0, jnp.stack([for_mine, for_theirs]), jnp.stack([for_theirs, for_mine])
    )
    parts = jnp.broadcast_to(halves[None], (n_xy, *halves.shape))
    part = exchange(parts.reshape(2 * n_xy, *halves.shape[1:]), DP).sum(axis=0)
    whole = to_each(part, "vocab").sum(axis=0)
    log_probs = whole[1] - jnp.log(whole[0])
    log_probs = lax.dynamic_slice_in_dim(log_probs, lax.axis_index(XY) * SLOTS, used)
    return (jnp.transpose(log_probs.reshape(STEPS, own_rows)), final_hidden)


def solution(mesh):
    finer = Mesh(
        mesh.devices.reshape(4, 4, 2, mesh.shape["vocab"]), ("dp_0", "dp_1", "dp_2", "vocab")
    )
    in_specs = (P(DP, None), P(), P(DP_VOCAB, None), P())
    out_specs = (P(DP, None), P(DP, None))
    return jax.shard_map(
        on_device, mesh=finer, in_specs=in_specs, out_specs=out_specs, check_vma=False
    )
```

```python
import functools
import math

import jax
import jax.numpy as jnp
from jax import lax
from jax.experimental import pallas as pl
from jax.experimental.pallas import tpu as pltpu
from jax.sharding import Mesh
from jax.sharding import PartitionSpec as P

D = 4608
STEPS = 3
XY = ("dp_0", "dp_1")
DP = ("dp_0", "dp_1", "dp_2")
DP_VOCAB = ("dp_0", "dp_1", "dp_2", "vocab")
PIECES = 4
SLOTS = 8

epsilon_value = 1e-06
softcap_value = 30.0


def exchange(x, axis):
    return lax.all_to_all(x, axis, split_axis=0, concat_axis=0, tiled=True)


def to_each(x, axis):
    return exchange(jnp.broadcast_to(x[None], (lax.axis_size(axis), *x.shape)), axis)


def other_core(x):
    return lax.ppermute(x, "dp_2", [(0, 1), (1, 0)])


def holder_of(token, shard_rows, n_devices):
    low = (shard_rows & -shard_rows).bit_length() - 1
    odd, limit = shard_rows >> low, shard_rows * n_devices >> low
    for shift in range(24):
        factor = (1 << shift) // odd + 1
        if limit * factor < 2**31 and all(
            x * factor >> shift == x // odd for x in range(limit + 1)
        ):
            return ((token >> low) * factor) >> shift
    return lax.div(token, jnp.full_like(token, shard_rows))


def parted(x, n):
    if n & (n - 1) == 0:
        return x >> (n.bit_length() - 1), x & (n - 1)
    n = jnp.full_like(x, n)
    return lax.div(x, n), lax.rem(x, n)


def key_of(holder, index, summary, own_rows, n_vocab):
    core = parted(summary, own_rows)[0] & 1
    return ((core * n_vocab + parted(holder, n_vocab)[1]) << 8) + index


def picked(block, index):
    rows = lax.broadcasted_iota(jnp.int32, block.shape, 0)
    return jnp.sum(jnp.where(rows == index, block.astype(jnp.float32), 0.0), axis=0, keepdims=True)


def placed(row, index, count):
    rows = lax.broadcasted_iota(jnp.int32, (count, row.shape[1]), 0)
    return jnp.where(rows == index, row, 0.0)


def in_pieces(row):
    width = row.shape[1] // PIECES
    parts = [placed(row[:, i * width : (i + 1) * width], i, PIECES) for i in range(PIECES)]
    return sum(parts[1:], parts[0])


def in_row(block):
    return jnp.concatenate([picked(block, i) for i in range(PIECES)], axis=1)


def split(hidden, out):
    count = hidden.shape[0]
    total = jnp.zeros((SLOTS, D), jnp.float32)
    rest = jnp.zeros((SLOTS, D // PIECES), jnp.float32)
    for row in range(count):
        state = hidden[row : row + 1, :]
        high = state.astype(jnp.bfloat16).astype(jnp.float32)
        total = total + placed(high, SLOTS - count + row, SLOTS)
        pieces = jnp.concatenate([in_pieces(state - high)] * (SLOTS // PIECES), axis=0)
        at = lax.broadcasted_iota(jnp.int32, pieces.shape, 0) // PIECES
        rest = rest + jnp.where(at == row, pieces, 0.0)
    out[:, :D] = total.astype(jnp.bfloat16)
    out[:, D:] = rest.astype(jnp.bfloat16)


def lookup_kernel(
    turn, tokens, tokens_again, hidden, table, rows, packed, rank_out, slots, held, found, sem
):
    steps, summaries = tokens.shape
    shard_rows, n_groups, n_vocab = table.shape[0], rows.shape[0], lax.axis_size("vocab")
    n_devices, own_rows = n_groups * n_vocab, hidden.shape[0]
    lines, vocab = n_groups // 2, lax.axis_index("vocab")
    start = (lax.axis_index(DP) * n_vocab + vocab) * shard_rows
    copy = pltpu.make_async_copy(table, held, sem)
    copy.start()
    rows[...] = jnp.zeros_like(rows)
    split(hidden, packed)
    summary_of = lax.broadcasted_iota(jnp.int32, tokens.shape, 1)
    index_of = lax.broadcasted_iota(jnp.int32, tokens.shape, 0) * summaries + summary_of
    holders = holder_of(tokens_again[...], shard_rows, n_devices)
    keys = key_of(holders, index_of, summary_of, own_rows, n_vocab)

    def scan(summary, state):
        n, rank, among = state
        for step in range(steps):
            token, index = tokens[step, summary], step * summaries + summary
            local = token - start
            found[n] = index
            n = n + ((local >= 0) & (local < shard_rows)).astype(jnp.int32)
            holder = holder_of(token, shard_rows, n_devices)
            key = key_of(holder, index, summary, own_rows, n_vocab)
            before = key < keys
            rank = rank + jnp.where(before, 1, 0)
            among = among + jnp.where(before & ((key ^ keys) < 256), 1, 0)
        return n, rank, among

    none = jnp.zeros(tokens.shape, jnp.int32)
    n, rank, among = lax.fori_loop(0, summaries, scan, (jnp.int32(0), none, none))
    rank_out[...] = rank
    turns = parted(among, lines)[0]
    first = lax.axis_index("dp_2") * (steps * summaries // 2) + lax.axis_index(XY)
    for i in range(slots.shape[1]):
        hit = rank == first + i * lines
        slots[0, i] = jnp.sum(jnp.where(hit, holders, 0))
        slots[1, i] = jnp.sum(jnp.where(hit, turns, 0))
        slots[2, i] = jnp.int32(0)
    slots[2, 0] = jnp.max(turns) + 1
    copy.wait()

    def give(i, _):
        index = found[i]
        step, summary = parted(index, summaries)
        local = tokens[step, summary] - start
        core = parted(summary, own_rows)[0] & 1
        at = index_of == index
        its_rank = jnp.sum(jnp.where(at, rank, 0)) - core * (steps * summaries // 2)
        its_turn = jnp.sum(jnp.where(at, turns, 0))

        @pl.when(its_turn == turn[0])
        def _():
            block = held[pl.ds(pl.multiple_of(local // 16 * 16, 16), 16), :]
            row = in_pieces(picked(block, local % 16))
            rows[parted(its_rank, lines)[1] * 2 + core] = row.astype(jnp.bfloat16)

        return 0

    lax.fori_loop(0, n, give, 0)


def relay_kernel(turn, slots, rows, out, buffer, sem):
    n_vocab = out.shape[0]
    out[...] = jnp.zeros_like(out)
    for i in range(slots.shape[1]):

        @pl.when((slots[0, i] % n_vocab == lax.axis_index("vocab")) & (slots[1, i] == turn[0]))
        def _():
            copy = pltpu.make_async_copy(rows.at[slots[0, i] // n_vocab], buffer, sem)
            copy.start()
            copy.wait()
            out[...] = jnp.broadcast_to(buffer[...][None], out.shape)


def pack_kernel(turn, slots, rows, before, out):
    total = before[:, :D].astype(jnp.float32)
    for i in range(slots.shape[1]):
        row = in_row(rows[slots[0, i] % rows.shape[0]])
        total = total + placed(row, jnp.where(slots[1, i] == turn[0], i, -1), out.shape[0])
    out[:, :D] = total.astype(jnp.bfloat16)
    out[:, D:] = before[:, D:]


def head_kernel(rows, own_hidden, gain, places, table, out, *more):
    *final, gain_in, places_in, held, normed, sems = more
    final = final[0] if final else None
    copies = [
        pltpu.make_async_copy(x, y, sems.at[i])
        for i, (x, y) in enumerate([(places, places_in), (gain, gain_in), (table, held)])
    ]
    for copy in copies:
        copy.start()
    own_rows = own_hidden.shape[0]
    count = rows.shape[0] // SLOTS * own_rows
    steps = normed.shape[0] // count
    at = lax.broadcasted_iota(jnp.int32, (rows.shape[0], count), 0)
    state = lax.broadcasted_iota(jnp.int32, (rows.shape[0], count), 1)
    block, state = state // own_rows * SLOTS, state % own_rows

    def taken(chosen, columns):
        return lax.dot_general(
            jnp.where(chosen, 1.0, 0.0).astype(jnp.bfloat16), rows[:, columns],
            (((0,), (0,)), ((), ())), preferred_element_type=jnp.float32,
        )

    high = taken(at == block + SLOTS - own_rows + state, slice(0, D))
    low = [
        taken(at == block + state * PIECES + i, slice(D, D + D // PIECES)) for i in range(PIECES)
    ]
    hidden = high + jnp.concatenate(low, axis=1)
    copies[0].wait()

    def looked_up(row, n):
        at = lax.broadcasted_iota(jnp.int32, (rows.shape[0], n), 0)
        return taken(at == places_in[row : row + 1, :n], slice(0, D))

    looked = looked_up(0, (steps - 1) * count)
    copies[1].wait()
    current = hidden
    for step in range(steps):
        square_mean = jnp.mean(current * current, axis=-1, keepdims=True)
        state = current * lax.rsqrt(square_mean + epsilon_value) * gain_in[...]
        normed[pl.ds(step * count, count), :] = state.astype(jnp.bfloat16)
        if step < steps - 1:
            current = current + math.sqrt(D) * looked[step * count : (step + 1) * count]
    copies[2].wait()
    logits = lax.dot_general(
        held[...], normed[...], (((1,), (1,)), ((), ())), preferred_element_type=jnp.float32
    )
    capped = softcap_value * jnp.tanh(logits / softcap_value)
    exp_total = jnp.sum(jnp.exp(capped), axis=0, keepdims=True)
    entry = lax.broadcasted_iota(jnp.int32, capped.shape, 0)
    ids = places_in[1:2, : steps * count]
    target = jnp.sum(jnp.where(entry == ids, capped, 0.0), axis=0, keepdims=True)
    out[...] = jnp.concatenate([exp_total, target], axis=0)
    if final is None:
        return
    own = looked_up(2, SLOTS)
    current = own_hidden[...]
    for step in range(steps):
        current = current + math.sqrt(D) * own[step * own_rows : (step + 1) * own_rows]
    final[...] = current


def on_chip(kernel, out_shape, scratch, *operands):
    operands = [x if isinstance(x, tuple) else (x, pltpu.VMEM) for x in operands]
    return pl.pallas_call(
        kernel,
        out_shape=out_shape,
        in_specs=[pl.BlockSpec(memory_space=space) for _, space in operands],
        out_specs=jax.tree.map(
            lambda x: pl.BlockSpec(memory_space=pltpu.SMEM if x.shape[0] == 3 and x.shape[1] < SLOTS else pltpu.VMEM),
            out_shape,
        ),
        scratch_shapes=scratch,
        compiler_params=pltpu.CompilerParams(vmem_limit_bytes=24 * 2**20),
    )(*(x for x, _ in operands))


def on_device(hidden, norm_gain, embed_table, tokens):
    own_rows = hidden.shape[0]
    shard_rows = embed_table.shape[0]
    n_xy, n_groups, n_vocab = lax.axis_size(XY), lax.axis_size(DP), lax.axis_size("vocab")
    chip, core, summaries = lax.axis_index(XY), lax.axis_index("dp_2"), tokens.shape[0]
    start = (lax.axis_index(DP) * n_vocab + lax.axis_index("vocab")) * shard_rows
    half = summaries // 2
    bf16, f32, i32 = jnp.bfloat16, jnp.float32, jnp.int32
    by_step = jnp.transpose(tokens)
    row_shape = (PIECES, D // PIECES)

    per_half = STEPS * half
    n_slots = per_half // n_xy

    def lookup(turn):
        return on_chip(
            lookup_kernel,
            (
                jax.ShapeDtypeStruct((n_groups, *row_shape), bf16),
                jax.ShapeDtypeStruct((SLOTS, D + D // PIECES), bf16),
                jax.ShapeDtypeStruct(by_step.shape, i32),
                jax.ShapeDtypeStruct((3, n_slots), i32),
            ),
            [
                pltpu.VMEM(embed_table.shape, bf16),
                pltpu.SMEM((STEPS * summaries + 1,), i32),
                pltpu.SemaphoreType.DMA,
            ],
            (turn, pltpu.SMEM),
            (by_step, pltpu.SMEM),
            by_step,
            hidden,
            (embed_table, pl.ANY),
        )

    first = jnp.zeros((1,), i32)
    rows, packed, rank, slots = lookup(first)
    turns = slots[2, 0]
    rows = exchange(rows, DP)

    def relay(turn, rows):
        return on_chip(
            relay_kernel,
            jax.ShapeDtypeStruct((n_vocab, *row_shape), bf16),
            [pltpu.VMEM(row_shape, bf16), pltpu.SemaphoreType.DMA],
            (turn, pltpu.SMEM),
            (slots, pltpu.SMEM),
            (rows, pl.ANY),
        )

    def pack(turn, rows, packed):
        return on_chip(
            pack_kernel,
            jax.ShapeDtypeStruct(packed.shape, bf16),
            [],
            (turn, pltpu.SMEM),
            (slots, pltpu.SMEM),
            rows,
            packed,
        )

    rows = relay(first, rows)
    rows, rank, flat, gain = lax.optimization_barrier((rows, rank, by_step, norm_gain))
    rows = exchange(rows, "vocab")
    gain = gain.reshape(1, D)

    def halves(x):
        x = jnp.transpose(x.reshape(STEPS, n_xy, 2, own_rows), (2, 0, 1, 3)).reshape(2, per_half)
        return jnp.where(core == 0, x, x[::-1])

    place = rank - jnp.where(rank < per_half, 0, per_half)
    slot, line = parted(place, n_xy)
    place = halves(line * SLOTS + slot)
    own = lax.dynamic_slice_in_dim(
        place[0].reshape(STEPS, half), chip * own_rows, own_rows, 1
    ).reshape(1, STEPS * own_rows)
    wide = n_xy * SLOTS

    def widened(x):
        return jnp.pad(x, ((0, 0), (0, wide - x.shape[1])), constant_values=-1)

    own = widened(jnp.concatenate([own, own]).reshape(2, -1)[:, : STEPS * own_rows])
    places = jnp.stack(
        [widened(place[:, : 2 * half]), widened(halves(flat - start)), own, own], axis=1
    )
    places_mine, places_theirs = places[0], places[1]
    rows, places_mine, places_theirs, gain = lax.optimization_barrier(
        (rows, places_mine, places_theirs, gain)
    )

    def further(state):
        turn = state[0][None]
        rows = exchange(relay(turn, exchange(lookup(turn)[0], DP)), "vocab")
        return state[0] + 1, pack(turn, rows, state[1])

    _, packed = lax.while_loop(
        lambda state: state[0] < turns, further, (jnp.int32(1), pack(first, rows, packed))
    )
    of_mine = to_each(packed, XY).reshape(wide, D + D // PIECES)
    of_theirs = other_core(of_mine)

    def totals(rows, places, *more):
        return on_chip(
            head_kernel,
            (jax.ShapeDtypeStruct((2, per_half), f32), *more),
            [
                pltpu.VMEM((1, D), f32),
                pltpu.VMEM(places.shape, i32),
                pltpu.VMEM(embed_table.shape, bf16),
                pltpu.VMEM((per_half, D), bf16),
                pltpu.SemaphoreType.DMA((3,)),
            ],
            rows,
            hidden,
            (gain, pl.ANY),
            (places, pl.ANY),
            (embed_table, pl.ANY),
        )

    for_mine, final_hidden = totals(
        of_mine, places_mine, jax.ShapeDtypeStruct(hidden.shape, f32)
    )
    (for_theirs,) = totals(of_theirs, places_theirs)

    both = jnp.where(
        core == 0, jnp.stack([for_mine, for_theirs]), jnp.stack([for_theirs, for_mine])
    )
    parts = jnp.broadcast_to(both[None], (n_xy, *both.shape))
    part = exchange(parts.reshape(2 * n_xy, *both.shape[1:]), DP).sum(axis=0)
    whole = to_each(part, "vocab").sum(axis=0)
    log_probs = (whole[1] - jnp.log(whole[0])).reshape(STEPS, half)
    log_probs = lax.dynamic_slice_in_dim(log_probs, chip * own_rows, own_rows, 1)
    return (jnp.transpose(log_probs), final_hidden)


def solution(mesh):
    finer = Mesh(
        mesh.devices.reshape(4, 4, 2, mesh.shape["vocab"]), ("dp_0", "dp_1", "dp_2", "vocab")
    )
    in_specs = (P(DP, None), P(), P(DP_VOCAB, None), P())
    out_specs = (P(DP, None), P(DP, None))
    return jax.shard_map(
        on_device, mesh=finer, in_specs=in_specs, out_specs=out_specs, check_vma=False
    )
```

```python
import functools
import math

import jax
import jax.numpy as jnp
from jax import lax
from jax.experimental import pallas as pl
from jax.experimental.pallas import tpu as pltpu
from jax.sharding import Mesh
from jax.sharding import PartitionSpec as P

D = 4608
STEPS = 3
XY = ("dp_0", "dp_1")
DP = ("dp_0", "dp_1", "dp_2")
DP_VOCAB = ("dp_0", "dp_1", "dp_2", "vocab")
PIECES = 4
BLOCKS = 4
SLOTS = 8

epsilon_value = 1e-06
softcap_value = 30.0


def exchange(x, axis):
    return lax.all_to_all(x, axis, split_axis=0, concat_axis=0, tiled=True)


def to_each(x, axis):
    return exchange(jnp.broadcast_to(x[None], (lax.axis_size(axis), *x.shape)), axis)


def other_core(x):
    return lax.ppermute(x, "dp_2", [(0, 1), (1, 0)])


def holder_of(token, shard_rows, n_devices):
    low = (shard_rows & -shard_rows).bit_length() - 1
    odd, limit = shard_rows >> low, shard_rows * n_devices >> low
    for shift in range(24):
        factor = (1 << shift) // odd + 1
        if limit * factor < 2**31 and all(
            x * factor >> shift == x // odd for x in range(limit + 1)
        ):
            return ((token >> low) * factor) >> shift
    return lax.div(token, jnp.full_like(token, shard_rows))


def parted(x, n):
    if n & (n - 1) == 0:
        return x >> (n.bit_length() - 1), x & (n - 1)
    n = jnp.full_like(x, n)
    return lax.div(x, n), lax.rem(x, n)


def key_of(holder, index, summary, own_rows, n_vocab):
    core = parted(summary, own_rows)[0] & 1
    return ((core * n_vocab + parted(holder, n_vocab)[1]) << 8) + index


def picked(block, index):
    rows = lax.broadcasted_iota(jnp.int32, block.shape, 0)
    return jnp.sum(jnp.where(rows == index, block.astype(jnp.float32), 0.0), axis=0, keepdims=True)


def placed(row, index, count):
    rows = lax.broadcasted_iota(jnp.int32, (count, row.shape[1]), 0)
    return jnp.where(rows == index, row, 0.0)


def in_pieces(row):
    width = row.shape[1] // PIECES
    parts = [placed(row[:, i * width : (i + 1) * width], i, PIECES) for i in range(PIECES)]
    return sum(parts[1:], parts[0])


def pieces_of(block, index):
    width = block.shape[1] // PIECES
    to = lax.broadcasted_iota(jnp.int32, (2 * PIECES, block.shape[0]), 0)
    of = lax.broadcasted_iota(jnp.int32, (2 * PIECES, block.shape[0]), 1)
    total = jnp.zeros((2 * PIECES, width), jnp.float32)
    for i in range(PIECES):
        total = total + jnp.dot(
            jnp.where((to == i) & (of == index), 1.0, 0.0).astype(jnp.bfloat16),
            block[:, i * width : (i + 1) * width],
            preferred_element_type=jnp.float32,
        )
    return total[:PIECES]


def in_row(block):
    return jnp.concatenate([picked(block, i) for i in range(PIECES)], axis=1)


def split(hidden, out):
    count = hidden.shape[0]
    total = jnp.zeros((SLOTS, D), jnp.float32)
    rest = jnp.zeros((SLOTS, D // PIECES), jnp.float32)
    for row in range(count):
        state = hidden[row : row + 1, :]
        high = state.astype(jnp.bfloat16).astype(jnp.float32)
        total = total + placed(high, SLOTS - count + row, SLOTS)
        pieces = jnp.concatenate([in_pieces(state - high)] * (SLOTS // PIECES), axis=0)
        at = lax.broadcasted_iota(jnp.int32, pieces.shape, 0) // PIECES
        rest = rest + jnp.where(at == row, pieces, 0.0)
    out[:, :D] = total.astype(jnp.bfloat16)
    out[:, D:] = rest.astype(jnp.bfloat16)


def token_keys(tokens, own_rows, shard_rows):
    steps, summaries = tokens.shape
    n_vocab = lax.axis_size("vocab")
    summary = lax.broadcasted_iota(jnp.int32, tokens.shape, 1)
    index = lax.broadcasted_iota(jnp.int32, tokens.shape, 0) * summaries + summary
    holder = holder_of(tokens[...], shard_rows, lax.axis_size(DP) * n_vocab)
    return holder, key_of(holder, index, summary, own_rows, n_vocab)


def lookup_kernel(own_rows, turn, tokens, tokens_again, table, rows, held, found, sems):
    steps, summaries = tokens.shape
    shard_rows, n_groups, n_vocab = table.shape[0], rows.shape[0], lax.axis_size("vocab")
    lines, vocab, blocks = n_groups // 2, lax.axis_index("vocab"), held.shape[0]
    start = (lax.axis_index(DP) * n_vocab + vocab) * shard_rows

    def scan(summary, n):
        for step in range(steps):
            local = tokens[step, summary] - start
            found[n] = step * summaries + summary
            n = n + ((local >= 0) & (local < shard_rows)).astype(jnp.int32)
        return n

    n = lax.fori_loop(0, summaries, scan, jnp.int32(0))

    def local_of(i):
        step, summary = parted(found[i], summaries)
        return tokens[step, summary] - start

    def fetch(i, at):
        first = pl.multiple_of(local_of(i) >> 4 << 4, 16)
        return pltpu.make_async_copy(table.at[pl.ds(first, 16), :], held.at[at], sems.at[at])

    def begin(first):
        for at in range(blocks):

            @pl.when(first + at < n)
            def _():
                fetch(first + at, at).start()

    begin(jnp.int32(0))
    rows[...] = jnp.zeros_like(rows)
    _, keys = token_keys(tokens_again, own_rows, shard_rows)

    def give(i, at):
        core = parted(parted(found[i], summaries)[1], own_rows)[0] & 1
        key = ((core * n_vocab + vocab) << 8) + found[i]
        before = keys < key
        rank = jnp.sum(jnp.where(before, 1, 0)) - core * (steps * summaries // 2)
        among = jnp.sum(jnp.where(before & ((keys ^ key) < 256), 1, 0))
        fetch(i, at).wait()

        @pl.when(parted(among, lines)[0] == turn[0])
        def _():
            row = pieces_of(held[at], local_of(i) & 15)
            rows[parted(rank, lines)[1] * 2 + core] = row.astype(jnp.bfloat16)

    def several(i, _):
        first = i * blocks
        pl.when(i > 0)(lambda: begin(first))
        for at in range(blocks):
            pl.when(first + at < n)(functools.partial(give, first + at, at))
        return 0

    lax.fori_loop(0, (n + blocks - 1) // blocks, several, 0)


def plan_kernel(shard_rows, tokens, hidden, packed, mine, theirs, slots):
    steps, summaries = tokens.shape
    own_rows, lines = hidden.shape[0], lax.axis_size(XY)
    split(hidden, packed)
    holders, keys = token_keys(tokens, own_rows, shard_rows)
    upright = jnp.transpose(keys)
    rank, among = [], []
    for step in range(steps):
        key = keys[step : step + 1, :]
        before = [upright[:, i : i + 1] < key for i in range(steps)]
        near = [(upright[:, i : i + 1] ^ key) < 256 for i in range(steps)]
        counts = sum(jnp.where(x, 1, 0) for x in before)
        rank.append(jnp.sum(counts, axis=0, keepdims=True))
        counts = sum(jnp.where(x & y, 1, 0) for x, y in zip(before, near))
        among.append(jnp.sum(counts, axis=0, keepdims=True))
    rank, among = jnp.concatenate(rank, axis=0), jnp.concatenate(among, axis=0)
    turns, core, per_half = parted(among, lines)[0], lax.axis_index("dp_2"), rank.size // 2
    for i in range(slots.shape[1]):
        hit = rank == core * per_half + lax.axis_index(XY) + i * lines
        slots[0, i] = jnp.sum(jnp.where(hit, holders, 0))
        slots[1, i] = jnp.sum(jnp.where(hit, turns, 0))
        slots[2, i] = jnp.int32(0)
    slots[2, 0] = jnp.max(turns) + 1

    slot, line = parted(jnp.where(rank < per_half, rank, rank - per_half), lines)
    start = (
        lax.axis_index(DP) * lax.axis_size("vocab") + lax.axis_index("vocab")
    ) * shard_rows
    local = tokens[...] - start
    entry = jnp.where((local >= 0) & (local < shard_rows), local + 1, 0)
    wide = mine.shape[1]
    source = lax.broadcasted_iota(jnp.int32, (summaries, wide), 0)
    lane = lax.broadcasted_iota(jnp.int32, (summaries, wide), 1)
    lanes = lax.broadcasted_iota(jnp.int32, (1, wide), 1)

    def chosen(values, summary, block):
        taken = jnp.dot(
            values.astype(jnp.float32),
            jnp.where(source == summary, 1.0, 0.0),
            preferred_element_type=jnp.float32,
        )
        at = [jnp.where(parted(lanes, block)[0] == i, taken[i : i + 1], 0.0) for i in range(steps)]
        return sum(at).astype(jnp.int32)

    half = summaries // 2
    own = lax.axis_index(DP) * own_rows + parted(lane, own_rows)[1]
    for out, its_core in ((mine, core), (theirs, 1 - core)):
        chip, row = parted(parted(lane, half)[1], own_rows)
        summary = (chip * 2 + its_core) * own_rows + row
        high, low = (chosen(x, summary, half) for x in (entry >> 4, entry & 15))
        place = line * SLOTS + slot
        out[...] = jnp.concatenate(
            [
                chosen(place, summary, half),
                (high << 4) + low - 1,
                chosen(place, own, own_rows),
                jnp.zeros((1, wide), jnp.int32),
            ],
            axis=0,
        )


def relay_kernel(turn, slots, rows, out, buffer, sem):
    out[...] = jnp.zeros_like(out)
    for i in range(slots.shape[1]):
        source, plane = parted(slots[0, i], out.shape[0])

        @pl.when((plane == lax.axis_index("vocab")) & (slots[1, i] == turn[0]))
        def _():
            copy = pltpu.make_async_copy(rows.at[source], buffer, sem)
            copy.start()
            copy.wait()
            out[...] = jnp.broadcast_to(buffer[...][None], out.shape)


def pack_kernel(turn, slots, rows, before, out):
    total = before[:, :D].astype(jnp.float32)
    for i in range(slots.shape[1]):
        row = in_row(rows[parted(slots[0, i], rows.shape[0])[1]])
        total = total + placed(row, jnp.where(slots[1, i] == turn[0], i, -1), out.shape[0])
    out[:, :D] = total.astype(jnp.bfloat16)
    out[:, D:] = before[:, D:]


def head_kernel(rows, own_hidden, gain, places, table, out, *more):
    *final, gain_in, places_in, held, normed, sems = more
    final = final[0] if final else None
    pairs = [(places, places_in), (gain, gain_in), (table, held)]
    copies = [
        pltpu.make_async_copy(x, y, sems.at[i])
        for i, (x, y) in enumerate(pairs if final is not None else pairs[:2])
    ]
    for copy in copies:
        copy.start()
    own_rows = own_hidden.shape[0]
    count = rows.shape[0] // SLOTS * own_rows
    steps = normed.shape[0] // count
    at = lax.broadcasted_iota(jnp.int32, (rows.shape[0], count), 0)
    state = lax.broadcasted_iota(jnp.int32, (rows.shape[0], count), 1)
    block, state = state // own_rows * SLOTS, state % own_rows

    def taken(chosen, columns):
        return lax.dot_general(
            jnp.where(chosen, 1.0, 0.0).astype(jnp.bfloat16), rows[:, columns],
            (((0,), (0,)), ((), ())), preferred_element_type=jnp.float32,
        )

    high = taken(at == block + SLOTS - own_rows + state, slice(0, D))
    low = [
        taken(at == block + state * PIECES + i, slice(D, D + D // PIECES)) for i in range(PIECES)
    ]
    hidden = high + jnp.concatenate(low, axis=1)
    copies[0].wait()

    def looked_up(row, n):
        at = lax.broadcasted_iota(jnp.int32, (rows.shape[0], n), 0)
        return taken(at == places_in[row : row + 1, :n], slice(0, D))

    looked = looked_up(0, (steps - 1) * count)
    copies[1].wait()
    current = hidden
    for step in range(steps):
        square_mean = jnp.mean(current * current, axis=-1, keepdims=True)
        state = current * lax.rsqrt(square_mean + epsilon_value) * gain_in[...]
        normed[pl.ds(step * count, count), :] = state.astype(jnp.bfloat16)
        if step < steps - 1:
            current = current + math.sqrt(D) * looked[step * count : (step + 1) * count]
    for copy in copies[2:]:
        copy.wait()
    logits = lax.dot_general(
        (held if copies[2:] else table)[...], normed[...], (((1,), (1,)), ((), ())), preferred_element_type=jnp.float32
    )
    capped = softcap_value * jnp.tanh(logits / softcap_value)
    exp_total = jnp.sum(jnp.exp(capped), axis=0, keepdims=True)
    entry = lax.broadcasted_iota(jnp.int32, capped.shape, 0)
    ids = places_in[1:2, : steps * count]
    target = jnp.sum(jnp.where(entry == ids, capped, 0.0), axis=0, keepdims=True)
    out[...] = jnp.concatenate([exp_total, target], axis=0)
    if final is None:
        return
    own = looked_up(2, SLOTS)
    current = own_hidden[...]
    for step in range(steps):
        current = current + math.sqrt(D) * own[step * own_rows : (step + 1) * own_rows]
    final[...] = current


def on_chip(kernel, out_shape, scratch, *operands, scalars=None, cost=None):
    operands = [x if isinstance(x, tuple) else (x, pltpu.VMEM) for x in operands]
    return pl.pallas_call(
        kernel,
        out_shape=out_shape,
        in_specs=[pl.BlockSpec(memory_space=space) for _, space in operands],
        out_specs=jax.tree.map(
            lambda x: pl.BlockSpec(memory_space=pltpu.SMEM if x is scalars else pltpu.VMEM),
            out_shape,
        ),
        scratch_shapes=scratch,
        cost_estimate=cost,
        compiler_params=pltpu.CompilerParams(vmem_limit_bytes=24 * 2**20),
    )(*(x for x, _ in operands))


def on_device(hidden, norm_gain, embed_table, tokens):
    own_rows = hidden.shape[0]
    shard_rows = embed_table.shape[0]
    n_xy, n_groups, n_vocab = lax.axis_size(XY), lax.axis_size(DP), lax.axis_size("vocab")
    chip, core, summaries = lax.axis_index(XY), lax.axis_index("dp_2"), tokens.shape[0]
    half = summaries // 2
    bf16, f32, i32 = jnp.bfloat16, jnp.float32, jnp.int32
    by_step = jnp.transpose(tokens)
    row_shape = (PIECES, D // PIECES)

    per_half = STEPS * half
    n_slots = per_half // n_xy

    def lookup(turn):
        return on_chip(
            functools.partial(lookup_kernel, own_rows),
            jax.ShapeDtypeStruct((n_groups, *row_shape), bf16),
            [
                pltpu.VMEM((BLOCKS, 16, D), bf16),
                pltpu.SMEM((STEPS * summaries + 1,), i32),
                pltpu.SemaphoreType.DMA((BLOCKS,)),
            ],
            (turn, pltpu.SMEM),
            (by_step, pltpu.SMEM),
            by_step,
            (embed_table, pl.ANY),
        )

    first = jnp.zeros((1,), i32)
    rows, shared, all_tokens, gain = lax.optimization_barrier(
        (lookup(first), hidden, by_step, norm_gain)
    )
    rows = exchange(rows, DP)
    wide = n_xy * SLOTS
    slots = jax.ShapeDtypeStruct((3, n_slots), i32)
    packed, places_mine, places_theirs, slots = on_chip(
        functools.partial(plan_kernel, shard_rows),
        (
            jax.ShapeDtypeStruct((SLOTS, D + D // PIECES), bf16),
            jax.ShapeDtypeStruct((4, wide), i32),
            jax.ShapeDtypeStruct((4, wide), i32),
            slots,
        ),
        [],
        all_tokens,
        shared,
        scalars=slots,
        cost=pl.CostEstimate(flops=0, bytes_accessed=2**23, transcendentals=0),
    )
    gain = gain.reshape(1, D)
    turns = slots[2, 0]
    rows, packed, places_mine, places_theirs, slots, turns, gain = lax.optimization_barrier(
        (rows, packed, places_mine, places_theirs, slots, turns, gain)
    )

    def relay(turn, rows):
        return on_chip(
            relay_kernel,
            jax.ShapeDtypeStruct((n_vocab, *row_shape), bf16),
            [pltpu.VMEM(row_shape, bf16), pltpu.SemaphoreType.DMA],
            (turn, pltpu.SMEM),
            (slots, pltpu.SMEM),
            (rows, pl.ANY),
        )

    def pack(turn, rows, packed):
        return on_chip(
            pack_kernel,
            jax.ShapeDtypeStruct(packed.shape, bf16),
            [],
            (turn, pltpu.SMEM),
            (slots, pltpu.SMEM),
            rows,
            packed,
        )

    rows = exchange(relay(first, rows), "vocab")

    def further(state):
        turn = state[0][None]
        rows = exchange(relay(turn, exchange(lookup(turn), DP)), "vocab")
        return state[0] + 1, pack(turn, rows, state[1])

    packed = lax.cond(
        turns > 1,
        lambda x: lax.while_loop(lambda state: state[0] < turns, further, (jnp.int32(1), x))[1],
        lambda x: x,
        pack(first, rows, packed),
    )
    of_mine = to_each(packed, XY).reshape(wide, D + D // PIECES)
    of_theirs = other_core(of_mine)

    def totals(rows, places, *more):
        return on_chip(
            head_kernel,
            (jax.ShapeDtypeStruct((2, per_half), f32), *more),
            [
                pltpu.VMEM((1, D), f32),
                pltpu.VMEM(places.shape, i32),
                pltpu.VMEM(embed_table.shape if more else (16, 128), bf16),
                pltpu.VMEM((per_half, D), bf16),
                pltpu.SemaphoreType.DMA((3,)),
            ],
            rows,
            hidden,
            (gain, pl.ANY),
            (places, pl.ANY),
            (embed_table, pl.ANY if more else pltpu.VMEM),
        )

    for_mine, final_hidden = totals(
        of_mine, places_mine, jax.ShapeDtypeStruct(hidden.shape, f32)
    )
    (for_theirs,) = totals(of_theirs, places_theirs)

    both = jnp.where(
        core == 0, jnp.stack([for_mine, for_theirs]), jnp.stack([for_theirs, for_mine])
    )
    parts = jnp.broadcast_to(both[None], (n_xy, *both.shape))
    part = exchange(parts.reshape(2 * n_xy, *both.shape[1:]), DP).sum(axis=0)
    whole = to_each(part, "vocab").sum(axis=0)
    log_probs = (whole[1] - jnp.log(whole[0])).reshape(STEPS, half)
    log_probs = lax.dynamic_slice_in_dim(log_probs, chip * own_rows, own_rows, 1)
    return (jnp.transpose(log_probs), final_hidden)


def solution(mesh):
    finer = Mesh(
        mesh.devices.reshape(4, 4, 2, mesh.shape["vocab"]), ("dp_0", "dp_1", "dp_2", "vocab")
    )
    in_specs = (P(DP, None), P(), P(DP_VOCAB, None), P())
    out_specs = (P(DP, None), P(DP, None))
    return jax.shard_map(
        on_device, mesh=finer, in_specs=in_specs, out_specs=out_specs, check_vma=False
    )
```

```python
import functools
import math

import jax
import jax.numpy as jnp
from jax import lax
from jax.experimental import pallas as pl
from jax.experimental.pallas import tpu as pltpu
from jax.sharding import Mesh
from jax.sharding import PartitionSpec as P

D = 4608
STEPS = 3
XY = ("dp_0", "dp_1")
DP = ("dp_0", "dp_1", "dp_2")
DP_VOCAB = ("dp_0", "dp_1", "dp_2", "vocab")
PIECES = 4
BLOCKS = 4
SLOTS = 8

epsilon_value = 1e-06
softcap_value = 30.0


def exchange(x, axis):
    return lax.all_to_all(x, axis, split_axis=0, concat_axis=0, tiled=True)


def to_each(x, axis):
    return exchange(jnp.broadcast_to(x[None], (lax.axis_size(axis), *x.shape)), axis)


def other_core(x):
    return lax.ppermute(x, "dp_2", [(0, 1), (1, 0)])


def holder_of(token, shard_rows, n_devices):
    low = (shard_rows & -shard_rows).bit_length() - 1
    odd, limit = shard_rows >> low, shard_rows * n_devices >> low
    for shift in range(24):
        factor = (1 << shift) // odd + 1
        if limit * factor < 2**31 and all(
            x * factor >> shift == x // odd for x in range(limit + 1)
        ):
            return ((token >> low) * factor) >> shift
    return lax.div(token, jnp.full_like(token, shard_rows))


def parted(x, n):
    if n & (n - 1) == 0:
        return x >> (n.bit_length() - 1), x & (n - 1)
    n = jnp.full_like(x, n)
    return lax.div(x, n), lax.rem(x, n)


def key_of(holder, index, summary, own_rows, n_vocab):
    core = parted(summary, own_rows)[0] & 1
    return ((core * n_vocab + parted(holder, n_vocab)[1]) << 8) + index


def picked(block, index):
    rows = lax.broadcasted_iota(jnp.int32, block.shape, 0)
    return jnp.sum(jnp.where(rows == index, block.astype(jnp.float32), 0.0), axis=0, keepdims=True)


def placed(row, index, count):
    rows = lax.broadcasted_iota(jnp.int32, (count, row.shape[1]), 0)
    return jnp.where(rows == index, row, 0.0)


def in_pieces(row):
    width = row.shape[1] // PIECES
    parts = [placed(row[:, i * width : (i + 1) * width], i, PIECES) for i in range(PIECES)]
    return sum(parts[1:], parts[0])


def pieces_of(block, index):
    width = block.shape[1] // PIECES
    to = lax.broadcasted_iota(jnp.int32, (2 * PIECES, block.shape[0]), 0)
    of = lax.broadcasted_iota(jnp.int32, (2 * PIECES, block.shape[0]), 1)
    total = jnp.zeros((2 * PIECES, width), jnp.float32)
    for i in range(PIECES):
        total = total + jnp.dot(
            jnp.where((to == i) & (of == index), 1.0, 0.0).astype(jnp.bfloat16),
            block[:, i * width : (i + 1) * width],
            preferred_element_type=jnp.float32,
        )
    return total[:PIECES]


def in_row(block):
    return jnp.concatenate([picked(block, i) for i in range(PIECES)], axis=1)


def split(hidden, out):
    count = hidden.shape[0]
    total = jnp.zeros((SLOTS, D), jnp.float32)
    rest = jnp.zeros((SLOTS, D // PIECES), jnp.float32)
    for row in range(count):
        state = hidden[row : row + 1, :]
        high = state.astype(jnp.bfloat16).astype(jnp.float32)
        total = total + placed(high, SLOTS - count + row, SLOTS)
        pieces = jnp.concatenate([in_pieces(state - high)] * (SLOTS // PIECES), axis=0)
        at = lax.broadcasted_iota(jnp.int32, pieces.shape, 0) // PIECES
        rest = rest + jnp.where(at == row, pieces, 0.0)
    out[:, :D] = total.astype(jnp.bfloat16)
    out[:, D:] = rest.astype(jnp.bfloat16)


def token_keys(tokens, own_rows, shard_rows):
    steps, summaries = tokens.shape
    n_vocab = lax.axis_size("vocab")
    summary = lax.broadcasted_iota(jnp.int32, tokens.shape, 1)
    index = lax.broadcasted_iota(jnp.int32, tokens.shape, 0) * summaries + summary
    holder = holder_of(tokens[...], shard_rows, lax.axis_size(DP) * n_vocab)
    return holder, key_of(holder, index, summary, own_rows, n_vocab)


def lookup_kernel(own_rows, turn, tokens, tokens_again, table, rows, held, found, sems):
    steps, summaries = tokens.shape
    shard_rows, n_groups, n_vocab = table.shape[0], rows.shape[0], lax.axis_size("vocab")
    lines, vocab, blocks = n_groups // 2, lax.axis_index("vocab"), held.shape[0]
    start = (lax.axis_index(DP) * n_vocab + vocab) * shard_rows

    def scan(summary, n):
        for step in range(steps):
            local = tokens[step, summary] - start
            found[n] = step * summaries + summary
            n = n + ((local >= 0) & (local < shard_rows)).astype(jnp.int32)
        return n

    n = lax.fori_loop(0, summaries, scan, jnp.int32(0))

    def local_of(i):
        step, summary = parted(found[i], summaries)
        return tokens[step, summary] - start

    def fetch(i, at):
        first = pl.multiple_of(local_of(i) >> 4 << 4, 16)
        return pltpu.make_async_copy(table.at[pl.ds(first, 16), :], held.at[at], sems.at[at])

    def begin(first):
        for at in range(blocks):

            @pl.when(first + at < n)
            def _():
                fetch(first + at, at).start()

    begin(jnp.int32(0))
    rows[...] = jnp.zeros_like(rows)
    _, keys = token_keys(tokens_again, own_rows, shard_rows)

    def give(i, at):
        core = parted(parted(found[i], summaries)[1], own_rows)[0] & 1
        key = ((core * n_vocab + vocab) << 8) + found[i]
        before = keys < key
        rank = jnp.sum(jnp.where(before, 1, 0)) - core * (steps * summaries // 2)
        among = jnp.sum(jnp.where(before & ((keys ^ key) < 256), 1, 0))
        fetch(i, at).wait()

        @pl.when(parted(among, lines)[0] == turn[0])
        def _():
            row = pieces_of(held[at], local_of(i) & 15)
            rows[parted(rank, lines)[1] * 2 + core] = row.astype(jnp.bfloat16)

    def several(i, _):
        first = i * blocks
        pl.when(i > 0)(lambda: begin(first))
        for at in range(blocks):
            pl.when(first + at < n)(functools.partial(give, first + at, at))
        return 0

    lax.fori_loop(0, (n + blocks - 1) // blocks, several, 0)


def plan_kernel(shard_rows, tokens, hidden, packed, mine, theirs, slots):
    steps, summaries = tokens.shape
    own_rows, lines = hidden.shape[0], lax.axis_size(XY)
    split(hidden, packed)
    holders, keys = token_keys(tokens, own_rows, shard_rows)
    upright = jnp.transpose(keys)
    rank, among = [], []
    for step in range(steps):
        key = keys[step : step + 1, :]
        before = [upright[:, i : i + 1] < key for i in range(steps)]
        near = [(upright[:, i : i + 1] ^ key) < 256 for i in range(steps)]
        counts = sum(jnp.where(x, 1, 0) for x in before)
        rank.append(jnp.sum(counts, axis=0, keepdims=True))
        counts = sum(jnp.where(x & y, 1, 0) for x, y in zip(before, near))
        among.append(jnp.sum(counts, axis=0, keepdims=True))
    rank, among = jnp.concatenate(rank, axis=0), jnp.concatenate(among, axis=0)
    turns, core, per_half = parted(among, lines)[0], lax.axis_index("dp_2"), rank.size // 2
    for i in range(slots.shape[1]):
        hit = rank == core * per_half + lax.axis_index(XY) + i * lines
        slots[0, i] = jnp.sum(jnp.where(hit, holders, 0))
        slots[1, i] = jnp.sum(jnp.where(hit, turns, 0))
        slots[2, i] = jnp.int32(0)
    slots[2, 0] = jnp.max(turns) + 1

    slot, line = parted(jnp.where(rank < per_half, rank, rank - per_half), lines)
    start = (
        lax.axis_index(DP) * lax.axis_size("vocab") + lax.axis_index("vocab")
    ) * shard_rows
    local = tokens[...] - start
    entry = jnp.where((local >= 0) & (local < shard_rows), local + 1, 0)
    wide = mine.shape[1]
    source = lax.broadcasted_iota(jnp.int32, (summaries, wide), 0)
    lane = lax.broadcasted_iota(jnp.int32, (summaries, wide), 1)
    lanes = lax.broadcasted_iota(jnp.int32, (1, wide), 1)

    def chosen(values, summary, block):
        taken = jnp.dot(
            values.astype(jnp.float32),
            jnp.where(source == summary, 1.0, 0.0),
            preferred_element_type=jnp.float32,
        )
        at = [jnp.where(parted(lanes, block)[0] == i, taken[i : i + 1], 0.0) for i in range(steps)]
        return sum(at).astype(jnp.int32)

    half = summaries // 2
    own = lax.axis_index(DP) * own_rows + parted(lane, own_rows)[1]
    for out, its_core in ((mine, core), (theirs, 1 - core)):
        chip, row = parted(parted(lane, half)[1], own_rows)
        summary = (chip * 2 + its_core) * own_rows + row
        high, low = (chosen(x, summary, half) for x in (entry >> 4, entry & 15))
        place = line * SLOTS + slot
        out[...] = jnp.concatenate(
            [
                chosen(place, summary, half),
                (high << 4) + low - 1,
                chosen(place, own, own_rows),
                jnp.zeros((1, wide), jnp.int32),
            ],
            axis=0,
        )


def relay_kernel(turn, slots, rows, out):
    out[...] = jnp.zeros_like(out)
    for i in range(slots.shape[1]):
        source, plane = parted(slots[0, i], out.shape[0])

        @pl.when((plane == lax.axis_index("vocab")) & (slots[1, i] == turn[0]))
        def _():
            out[...] = jnp.broadcast_to(rows[source][None], out.shape)


def pack_kernel(turn, slots, rows, before, out):
    total = before[:, :D].astype(jnp.float32)
    for i in range(slots.shape[1]):
        row = in_row(rows[parted(slots[0, i], rows.shape[0])[1]])
        total = total + placed(row, jnp.where(slots[1, i] == turn[0], i, -1), out.shape[0])
    out[:, :D] = total.astype(jnp.bfloat16)
    out[:, D:] = before[:, D:]


def head_kernel(rows, own_hidden, gain, places, table, out, *more):
    *final, gain_in, places_in, held, normed, sems = more
    final = final[0] if final else None
    pairs = [(places, places_in), (gain, gain_in), (table, held)]
    copies = [
        pltpu.make_async_copy(x, y, sems.at[i])
        for i, (x, y) in enumerate(pairs if final is not None else pairs[:2])
    ]
    for copy in copies:
        copy.start()
    own_rows = own_hidden.shape[0]
    count = rows.shape[0] // SLOTS * own_rows
    steps = normed.shape[0] // count
    at = lax.broadcasted_iota(jnp.int32, (rows.shape[0], count), 0)
    state = lax.broadcasted_iota(jnp.int32, (rows.shape[0], count), 1)
    block, state = state // own_rows * SLOTS, state % own_rows

    def taken(chosen, columns):
        return lax.dot_general(
            jnp.where(chosen, 1.0, 0.0).astype(jnp.bfloat16), rows[:, columns],
            (((0,), (0,)), ((), ())), preferred_element_type=jnp.float32,
        )

    high = taken(at == block + SLOTS - own_rows + state, slice(0, D))
    low = [
        taken(at == block + state * PIECES + i, slice(D, D + D // PIECES)) for i in range(PIECES)
    ]
    hidden = high + jnp.concatenate(low, axis=1)
    copies[0].wait()

    def looked_up(row, n):
        at = lax.broadcasted_iota(jnp.int32, (rows.shape[0], n), 0)
        return taken(at == places_in[row : row + 1, :n], slice(0, D))

    looked = looked_up(0, (steps - 1) * count)
    copies[1].wait()
    current = hidden
    for step in range(steps):
        square_mean = jnp.mean(current * current, axis=-1, keepdims=True)
        state = current * lax.rsqrt(square_mean + epsilon_value) * gain_in[...]
        normed[pl.ds(step * count, count), :] = state.astype(jnp.bfloat16)
        if step < steps - 1:
            current = current + math.sqrt(D) * looked[step * count : (step + 1) * count]
    for copy in copies[2:]:
        copy.wait()
    logits = lax.dot_general(
        (held if copies[2:] else table)[...], normed[...], (((1,), (1,)), ((), ())), preferred_element_type=jnp.float32
    )
    capped = softcap_value * jnp.tanh(logits / softcap_value)
    exp_total = jnp.sum(jnp.exp(capped), axis=0, keepdims=True)
    entry = lax.broadcasted_iota(jnp.int32, capped.shape, 0)
    ids = places_in[1:2, : steps * count]
    target = jnp.sum(jnp.where(entry == ids, capped, 0.0), axis=0, keepdims=True)
    out[...] = jnp.concatenate([exp_total, target], axis=0)
    if final is None:
        return
    own = looked_up(2, SLOTS)
    current = own_hidden[...]
    for step in range(steps):
        current = current + math.sqrt(D) * own[step * own_rows : (step + 1) * own_rows]
    final[...] = current


def on_chip(kernel, out_shape, scratch, *operands, scalars=None, cost=None):
    operands = [x if isinstance(x, tuple) else (x, pltpu.VMEM) for x in operands]
    return pl.pallas_call(
        kernel,
        out_shape=out_shape,
        in_specs=[pl.BlockSpec(memory_space=space) for _, space in operands],
        out_specs=jax.tree.map(
            lambda x: pl.BlockSpec(memory_space=pltpu.SMEM if x is scalars else pltpu.VMEM),
            out_shape,
        ),
        scratch_shapes=scratch,
        cost_estimate=cost,
        compiler_params=pltpu.CompilerParams(vmem_limit_bytes=24 * 2**20),
    )(*(x for x, _ in operands))


def on_device(hidden, norm_gain, embed_table, tokens):
    own_rows = hidden.shape[0]
    shard_rows = embed_table.shape[0]
    n_xy, n_groups, n_vocab = lax.axis_size(XY), lax.axis_size(DP), lax.axis_size("vocab")
    chip, core, summaries = lax.axis_index(XY), lax.axis_index("dp_2"), tokens.shape[0]
    half = summaries // 2
    bf16, f32, i32 = jnp.bfloat16, jnp.float32, jnp.int32
    by_step = jnp.transpose(tokens)
    row_shape = (PIECES, D // PIECES)

    per_half = STEPS * half
    n_slots = per_half // n_xy

    def lookup(turn):
        return on_chip(
            functools.partial(lookup_kernel, own_rows),
            jax.ShapeDtypeStruct((n_groups, *row_shape), bf16),
            [
                pltpu.VMEM((BLOCKS, 16, D), bf16),
                pltpu.SMEM((STEPS * summaries + 1,), i32),
                pltpu.SemaphoreType.DMA((BLOCKS,)),
            ],
            (turn, pltpu.SMEM),
            (by_step, pltpu.SMEM),
            by_step,
            (embed_table, pl.ANY),
        )

    first = jnp.zeros((1,), i32)
    rows, shared, all_tokens, gain = lax.optimization_barrier(
        (lookup(first), hidden, by_step, norm_gain)
    )
    rows = exchange(rows, DP)
    wide = n_xy * SLOTS
    slots = jax.ShapeDtypeStruct((3, n_slots), i32)
    packed, places_mine, places_theirs, slots = on_chip(
        functools.partial(plan_kernel, shard_rows),
        (
            jax.ShapeDtypeStruct((SLOTS, D + D // PIECES), bf16),
            jax.ShapeDtypeStruct((4, wide), i32),
            jax.ShapeDtypeStruct((4, wide), i32),
            slots,
        ),
        [],
        all_tokens,
        shared,
        scalars=slots,
        cost=pl.CostEstimate(flops=0, bytes_accessed=2**23, transcendentals=0),
    )
    gain = gain.reshape(1, D)
    turns = slots[2, 0]
    rows, packed, places_mine, places_theirs, slots, turns, gain = lax.optimization_barrier(
        (rows, packed, places_mine, places_theirs, slots, turns, gain)
    )

    def relay(turn, rows):
        return on_chip(
            relay_kernel,
            jax.ShapeDtypeStruct((n_vocab, *row_shape), bf16),
            [],
            (turn, pltpu.SMEM),
            (slots, pltpu.SMEM),
            rows,
        )

    def pack(turn, rows, packed):
        return on_chip(
            pack_kernel,
            jax.ShapeDtypeStruct(packed.shape, bf16),
            [],
            (turn, pltpu.SMEM),
            (slots, pltpu.SMEM),
            rows,
            packed,
        )

    rows = exchange(relay(first, rows), "vocab")

    def further(state):
        turn = state[0][None]
        rows = exchange(relay(turn, exchange(lookup(turn), DP)), "vocab")
        return state[0] + 1, pack(turn, rows, state[1])

    packed = lax.cond(
        turns > 1,
        lambda x: lax.while_loop(lambda state: state[0] < turns, further, (jnp.int32(1), x))[1],
        lambda x: x,
        pack(first, rows, packed),
    )
    of_mine = to_each(packed, XY).reshape(wide, D + D // PIECES)
    of_theirs = other_core(of_mine)

    def totals(rows, places, *more):
        return on_chip(
            head_kernel,
            (jax.ShapeDtypeStruct((2, per_half), f32), *more),
            [
                pltpu.VMEM((1, D), f32),
                pltpu.VMEM(places.shape, i32),
                pltpu.VMEM(embed_table.shape if more else (16, 128), bf16),
                pltpu.VMEM((per_half, D), bf16),
                pltpu.SemaphoreType.DMA((3,)),
            ],
            rows,
            hidden,
            (gain, pl.ANY),
            (places, pl.ANY),
            (embed_table, pl.ANY if more else pltpu.VMEM),
        )

    for_mine, final_hidden = totals(
        of_mine, places_mine, jax.ShapeDtypeStruct(hidden.shape, f32)
    )
    (for_theirs,) = totals(of_theirs, places_theirs)

    both = jnp.where(
        core == 0, jnp.stack([for_mine, for_theirs]), jnp.stack([for_theirs, for_mine])
    )
    parts = jnp.broadcast_to(both[None], (n_xy, *both.shape))
    part = exchange(parts.reshape(2 * n_xy, *both.shape[1:]), DP).sum(axis=0)
    whole = to_each(part, "vocab").sum(axis=0)
    log_probs = (whole[1] - jnp.log(whole[0])).reshape(STEPS, half)
    log_probs = lax.dynamic_slice_in_dim(log_probs, chip * own_rows, own_rows, 1)
    return (jnp.transpose(log_probs), final_hidden)


def solution(mesh):
    finer = Mesh(
        mesh.devices.reshape(4, 4, 2, mesh.shape["vocab"]), ("dp_0", "dp_1", "dp_2", "vocab")
    )
    in_specs = (P(DP, None), P(), P(DP_VOCAB, None), P())
    out_specs = (P(DP, None), P(DP, None))
    return jax.shard_map(
        on_device, mesh=finer, in_specs=in_specs, out_specs=out_specs, check_vma=False
    )
```
